32 devices in a mesh: tiles: 32 (over z, y, x, core).
Axes of the slice: x: 2, y: 2, z: 4, core: 2. Of those that a mesh axis runs over, the one named last changes fastest.
Arguments:
- queries: bfloat16 [4096, 1536], P('tiles'), may hold values from -35 to 35
- keys: bfloat16 [4096, 1536], P('tiles'), may hold values from -4.1 to 4.1
- values: bfloat16 [4096, 1536], P('tiles'), may hold values from -4 to 4
- destination: int32 [4096], P('tiles'), may hold values from 0 to 4095, as said below
- row_clip: int32 [4096], P('tiles'), may hold values from 0 to 7, as said below
- residual: bfloat16 [4096, 3072], P('tiles'), may hold values from -3 to 3
- gate: float32 [8, 3072], replicated, may hold values from 0.5 to 2.5
- out_weight: bfloat16 [1536, 3072], replicated, may hold values from -0.15625 to 0.15625
Outputs:
- block_output: bfloat16 [4096, 3072], P('tiles')
The draws below stay inside these ranges and needn't reach their ends.
Inputs may be any that keep to these rules, and one draw needn't show every extreme that they name: `destination`: a permutation of the 4096 tile positions; position p is held by device p // 128; the rows of one device send at most 8 rows to one device, and some pair reaches 8 in every draw. `row_clip`: in tile order (row r at position destination[r]) every clip takes one contiguous run of positions, clips numbered in increasing order.
All inputs are finite; a program needn't handle non-finite values.
Results may differ from the reference program's by a relative error of at most 0.0027.
Values may be sent and summed in bfloat16 or wider, within the bound.
A program may use at most 64 MiB of HBM per device.

```python
import math
import jax
import jax.numpy as jnp
from jax import lax

D = 3072
HEADS = 12
HEAD_DIM = 128
TOK_DEV = 128
TOKENS = 4096
CLIPS = 8


def destination_plan(key):
    tile_rows = TOK_DEV
    peer_count = TOKENS // TOK_DEV
    mean_count = tile_rows // peer_count
    half_count = peer_count // 2
    key_shift, key_order, key_slots, key_rows = jax.random.split(key, 4)
    shift_vals = jax.random.randint(key_shift, (half_count,), -mean_count, mean_count + 1)
    shift_vals = shift_vals.at[0].set(mean_count)
    offset_counts = jnp.concatenate([mean_count + shift_vals, mean_count - shift_vals]).astype(jnp.int32)
    tile_order = jax.random.permutation(key_order, peer_count)
    sources = jnp.arange(peer_count)
    pair_counts = offset_counts[(tile_order[None, :] - sources[:, None]) % peer_count]
    running = jnp.cumsum(pair_counts, axis=1)
    run_start = running - pair_counts
    prior_rows = jnp.cumsum(pair_counts, axis=0) - pair_counts
    position = jnp.arange(tile_rows)
    target = jnp.sum((running[:, None, :] <= position[None, :, None]).astype(jnp.int32), axis=2)
    rank_index = position[None, :] - jnp.take_along_axis(run_start, target, axis=1)
    offset = jnp.take_along_axis(prior_rows, target, axis=1) + rank_index
    slot_orders = jax.vmap(lambda subkey: jax.random.permutation(subkey, tile_rows))(jax.random.split(key_slots, peer_count))
    slot_index = slot_orders[target, offset]
    placed = target * tile_rows + slot_index
    row_orders = jax.vmap(lambda subkey: jax.random.permutation(subkey, tile_rows))(jax.random.split(key_rows, peer_count))
    shuffled = jnp.take_along_axis(placed, row_orders, axis=1)
    return shuffled.reshape(-1).astype(jnp.int32)


def clip_plan(key):
    boundaries = jnp.sort(jax.random.permutation(key, TOKENS - 1)[:CLIPS - 1] + 1)
    return jnp.searchsorted(boundaries, jnp.arange(TOKENS), side='right').astype(jnp.int32)


def tile_pairs(key):
    feature_width = HEADS * HEAD_DIM
    tile_queries = jnp.clip(jax.random.normal(jax.random.fold_in(key, 13), (TOKENS, feature_width), jnp.float32), -4.0, 4.0)
    tile_keys = jnp.clip(jax.random.normal(jax.random.fold_in(key, 14), (TOKENS, feature_width), jnp.float32), -4.0, 4.0)
    return (tile_queries, tile_keys)


def draw_destination(key, part):
    return destination_plan(jax.random.fold_in(key, 11))


def draw_row_clip(key, part):
    placed = destination_plan(jax.random.fold_in(key, 11))
    return clip_plan(jax.random.fold_in(key, 12))[placed]


def draw_queries(key, part):
    placed = destination_plan(jax.random.fold_in(key, 11))
    return tile_pairs(key)[0][placed].astype(jnp.bfloat16)


def draw_keys(key, part):
    placed = destination_plan(jax.random.fold_in(key, 11))
    return tile_pairs(key)[1][placed].astype(jnp.bfloat16)


def levels(key, shape, cuts, low, top_value):
    def one(dim, parts):
        heights = jax.random.uniform(jax.random.fold_in(jax.random.fold_in(key, 6), dim), (parts,), jnp.float32, low / len(cuts), top_value / len(cuts))
        return jnp.repeat(jnp.exp(heights), shape[dim] // parts).reshape((-1,) + (1,) * (len(shape) - dim - 1))

    level = one(*cuts[0])
    for cut in cuts[1:]:
        level = level * one(*cut)
    return level


def normal_values(own_key, dims, deviation, reach, shards=(), kind=jnp.bfloat16):
    array = jax.random.normal(own_key, dims, jnp.float32) * deviation
    if len(shards) > 0:
        array = levels(own_key, dims, shards, -0.22, 0.18) * array
    return jnp.clip(array, min=-reach, max=reach).astype(kind)


def setup_inputs(seed: int = 0) -> dict:
    key_of = jax.random.split(jax.random.key(seed), 9)
    queries = draw_queries(jax.random.fold_in(key_of[8], 71), 0)
    keys = draw_keys(jax.random.fold_in(key_of[8], 71), 0)
    values = normal_values(key_of[2], (TOKENS, HEADS * HEAD_DIM), 1.0, 4.0, ((0, 32),))
    destination = draw_destination(jax.random.fold_in(key_of[8], 71), 0)
    row_clip = draw_row_clip(jax.random.fold_in(key_of[8], 71), 0)
    residual = normal_values(key_of[5], (TOKENS, D), 0.5, 3.0, ((0, 32),))
    gate = jnp.clip(jax.random.uniform(key_of[6], (CLIPS, D), jnp.float32, 0.5, 2.5), 0.5, 2.5)
    out_weight = normal_values(key_of[7], (HEADS * HEAD_DIM, D), (HEADS * HEAD_DIM) ** -0.5, 0.15625)
    return dict(queries=queries, keys=keys, values=values, destination=destination, row_clip=row_clip, residual=residual, gate=gate, out_weight=out_weight)


def attend_heads(tile_queries, tile_keys, tile_values, query_clip, key_clip):
    head_count = tile_queries.shape[1] // HEAD_DIM
    softmax_scale = 1.0 / math.sqrt(HEAD_DIM)
    same_clip = query_clip[:, None] == key_clip[None, :]

    def one_head(operands):
        query_head, key_head, value_head = operands
        scores = lax.dot_general(query_head, key_head, (((1,), (1,)), ((), ())), preferred_element_type=jnp.float32) * softmax_scale
        scores = jnp.where(same_clip, scores, -1e+30)
        row_max = lax.optimization_barrier(jnp.max(scores, axis=1, keepdims=True))
        weights = jnp.exp(scores - row_max)
        denominator = lax.optimization_barrier(jnp.sum(weights, axis=1, keepdims=True))
        probabilities = weights.astype(jnp.bfloat16)
        mixture = jnp.dot(probabilities, value_head, preferred_element_type=jnp.float32) / denominator
        return mixture.astype(jnp.bfloat16)

    def split_heads(matrix):
        return matrix.reshape(matrix.shape[0], head_count, HEAD_DIM).transpose(1, 0, 2)
    attended = lax.map(one_head, (split_heads(tile_queries), split_heads(tile_keys), split_heads(tile_values)))
    return attended.transpose(1, 0, 2).reshape(tile_queries.shape[0], -1)

def finish(attended, residual, query_clip, gate, out_weight):
    projected = jnp.dot(attended, out_weight, preferred_element_type=jnp.float32)
    lookup = (query_clip[:, None] == jnp.arange(gate.shape[0], dtype=jnp.int32)[None, :]).astype(jnp.float32)
    gate_rows = jnp.dot(lookup, gate, precision=lax.Precision.HIGHEST)
    return (residual.astype(jnp.float32) + gate_rows * projected).astype(jnp.bfloat16)

def reference(queries, keys, values, destination, row_clip, residual, gate, out_weight):
    tiled = [jnp.zeros_like(source_array).at[destination].set(source_array) for source_array in (queries, keys, values, row_clip)]
    group_rows = 4 * TOK_DEV

    def one_group(group_index):
        row_start = group_index * group_rows
        pieces = [lax.dynamic_slice_in_dim(full_array, row_start, group_rows, 0) for full_array in tiled + [residual]]
        attended = attend_heads(pieces[0], pieces[1], pieces[2], pieces[3], pieces[3])
        return finish(attended, pieces[4], pieces[3], gate, out_weight)
    blocks = lax.map(one_group, jnp.arange(TOKENS // group_rows, dtype=jnp.int32))
    return blocks.reshape(TOKENS, -1)
```

```python
import functools
import math

import jax
import jax.numpy as jnp
from jax import lax
from jax.experimental import pallas as pl
from jax.experimental.pallas import tpu as pltpu
from jax.sharding import PartitionSpec as P

HEAD_DIM = 128
GROUP = 4
MESH = pl.DeviceIdType.MESH
F32 = jnp.float32
BF16 = jnp.bfloat16


def kernel(
    n,
    slots,
    q_ref,
    k_ref,
    v_ref,
    dest_ref,
    clip_ref,
    gate_ref,
    residual_hbm,
    weight_hbm,
    out_ref,
    send,
    recv,
    meta_send,
    meta_recv,
    pick,
    clip_col,
    bias,
    att_send,
    att,
    total,
    gate_rows,
    weight,
    residual,
    send_sem,
    recv_sem,
    meta_send_sem,
    meta_recv_sem,
    back_send_sem,
    back_recv_sem,
    load_sem,
    own_sem,
):
    tile = q_ref.shape[0]
    chunks = q_ref.shape[1] // (GROUP * HEAD_DIM)
    wide = GROUP * HEAD_DIM
    window = GROUP * tile
    windows = n // GROUP
    me = lax.axis_index("tiles")
    my_window = me // GROUP
    mine = me % GROUP

    barrier = pltpu.get_barrier_semaphore()

    def greet(o, carry):
        pl.semaphore_signal(barrier, inc=1, device_id=((me + o) % n,), device_id_type=MESH)
        return carry

    lax.fori_loop(1, n, greet, 0)

    load_weight = pltpu.make_async_copy(weight_hbm, weight, load_sem.at[0])
    load_residual = pltpu.make_async_copy(residual_hbm, residual, load_sem.at[1])

    dest_row = dest_ref[...]
    win_row = lax.div(dest_row, jnp.int32(window))
    code_row = lax.rem(dest_row, jnp.int32(window)) + 1 + clip_ref[...] * 1024
    line = lax.broadcasted_iota(jnp.int32, (tile, tile), 0)
    lane = lax.broadcasted_iota(jnp.int32, (tile, tile), 1)
    eye = line == lane

    def to_column(row):
        wide_row = jnp.broadcast_to(row.astype(F32), (tile, tile))
        return jnp.sum(jnp.where(eye, wide_row, 0.0), axis=1, keepdims=True).astype(jnp.int32)

    win_col = to_column(win_row)
    code_col = to_column(code_row)
    same = win_col == win_row
    rank_row = jnp.sum(jnp.where(same & (line < lane), 1.0, 0.0), axis=0, keepdims=True)
    rank_col = jnp.sum(jnp.where(same & (lane < line), 1.0, 0.0), axis=1, keepdims=True)
    slot_row = win_row * slots + rank_row.astype(jnp.int32)
    slot_col = win_col * 128 + rank_col.astype(jnp.int32)

    spread = lax.broadcasted_iota(jnp.int32, (tile, 128), 1) % slots
    for w in range(windows):
        hit = slot_col == spread + w * 128
        codes = jnp.sum(jnp.where(hit, code_col.astype(F32), 0.0), axis=0, keepdims=True)
        meta_send[w] = codes.astype(jnp.int32)

    slot_line = lax.broadcasted_iota(jnp.int32, (windows * slots, tile), 0)
    place = jnp.where(slot_line == slot_row, 1.0, 0.0).astype(BF16)

    def order(i):
        return n // 2 + (1 - 2 * (i % 2)) * ((i + 1) // 2)

    def meta_copy(o):
        to = (me + o) % n
        return pltpu.make_async_remote_copy(
            src_ref=meta_send.at[to // GROUP],
            dst_ref=meta_recv.at[me],
            send_sem=meta_send_sem.at[o],
            recv_sem=meta_recv_sem.at[me],
            device_id=(to,),
            device_id_type=MESH,
        )

    def meta_arrival(o):
        come = (me + o) % n
        return pltpu.make_async_remote_copy(
            src_ref=meta_send.at[0],
            dst_ref=meta_recv.at[come],
            send_sem=meta_send_sem.at[o],
            recv_sem=meta_recv_sem.at[come],
            device_id=(come,),
            device_id_type=MESH,
        )

    def copy(c, o):
        to = (me + o) % n
        return pltpu.make_async_remote_copy(
            src_ref=send.at[c, to // GROUP, to % GROUP],
            dst_ref=recv.at[c, me],
            send_sem=send_sem.at[c, o],
            recv_sem=recv_sem.at[c, me],
            device_id=(to,),
            device_id_type=MESH,
        )

    def arrival(c, o):
        come = (me + o) % n
        return pltpu.make_async_remote_copy(
            src_ref=send.at[c, 0, 0],
            dst_ref=recv.at[c, come],
            send_sem=send_sem.at[c, o],
            recv_sem=recv_sem.at[c, come],
            device_id=(come,),
            device_id_type=MESH,
        )

    def own_copy(c):
        return pltpu.make_async_copy(
            send.at[c, my_window, mine], recv.at[c, me], own_sem.at[c]
        )

    own_meta = pltpu.make_async_copy(meta_send.at[my_window], meta_recv.at[me], own_sem.at[chunks])

    for c in range(chunks):
        for t, ref in enumerate((q_ref, k_ref, v_ref)):
            packed = jnp.dot(
                place, ref[:, c * wide : (c + 1) * wide], preferred_element_type=F32
            ).astype(BF16)
            for j in range(GROUP):
                part = packed[:, j * HEAD_DIM : (j + 1) * HEAD_DIM]
                send[c, :, j, :, t * HEAD_DIM : (t + 1) * HEAD_DIM] = part.reshape(
                    windows, slots, HEAD_DIM
                )
        if c == 0:
            pl.semaphore_wait(barrier, n - 1)

            def start_meta(i, carry):
                meta_copy(order(i)).start()
                return carry

            lax.fori_loop(0, n - 1, start_meta, 0)
            own_meta.start()

        def start_chunk(i, carry, c=c):
            copy(c, order(i)).start()
            return carry

        lax.fori_loop(0, n - 1, start_chunk, 0)
        own_copy(c).start()

    load_weight.start()
    load_residual.start()

    def wait_meta(o, carry):
        meta_arrival(o).wait_recv()
        return carry

    lax.fori_loop(1, n, wait_meta, 0)
    own_meta.wait()
    per_row = 128 // slots
    lane_block = lax.broadcasted_iota(jnp.int32, (1, 128), 1) // slots
    rows = []
    for g in range(n // per_row):
        row = jnp.zeros((1, 128), jnp.int32)
        for i in range(per_row):
            row = jnp.where(lane_block == i, meta_recv[g * per_row + i], row)
        rows.append(row)
    for b in range(GROUP):
        spot = lax.broadcasted_iota(jnp.int32, (tile, 128), 0) + (b * tile + 1)
        sums = jnp.zeros((tile, 128), F32)
        for g, row in enumerate(rows):
            hit = spot == (row & 1023)
            pick[b * tile : (b + 1) * tile, g * 128 : (g + 1) * 128] = jnp.where(
                hit, 1.0, 0.0
            ).astype(BF16)
            sums = sums + jnp.where(hit, (row >> 10).astype(F32), 0.0)
        column = jnp.sum(sums, axis=1, keepdims=True)
        clip_col[b * tile : (b + 1) * tile, :] = jnp.broadcast_to(column, (tile, 128))
    for b in range(GROUP):
        key_clip = jnp.sum(
            jnp.where(eye, clip_col[b * tile : (b + 1) * tile, :], 0.0), axis=0, keepdims=True
        )
        for a in range(GROUP):
            query_clip = clip_col[a * tile : (a + 1) * tile, :]
            bias[a * tile : (a + 1) * tile, b * tile : (b + 1) * tile] = jnp.where(
                query_clip == key_clip, 0.0, -1e30
            )

    clips = gate_ref.shape[0]
    my_clip = clip_col[pl.ds(pl.multiple_of(mine * tile, tile), tile), :]
    lookup = jnp.where(
        my_clip[:, :clips] == lax.broadcasted_iota(jnp.int32, (tile, clips), 1).astype(F32), 1.0, 0.0
    )
    width = out_ref.shape[1]
    for x in range(0, width, 512):
        gate_rows[:, x : x + 512] = jnp.dot(
            lookup,
            gate_ref[:, x : x + 512],
            precision=lax.Precision.HIGHEST,
            preferred_element_type=F32,
        )
    load_weight.wait()
    load_residual.wait()

    def back_copy(c, o):
        to = (mine + o) % GROUP
        return pltpu.make_async_remote_copy(
            src_ref=att_send.at[c, to],
            dst_ref=att.at[c, mine],
            send_sem=back_send_sem.at[c, o],
            recv_sem=back_recv_sem.at[c, mine],
            device_id=(my_window * GROUP + to,),
            device_id_type=MESH,
        )

    def back_arrival(c, o):
        come = (mine + o) % GROUP
        return pltpu.make_async_remote_copy(
            src_ref=att_send.at[c, 0],
            dst_ref=att.at[c, come],
            send_sem=back_send_sem.at[c, o],
            recv_sem=back_recv_sem.at[c, come],
            device_id=(my_window * GROUP + come,),
            device_id_type=MESH,
        )

    def project(c):
        for o in range(1, GROUP):
            back_arrival(c, o).wait_recv()
        own_back(c).wait()
        attended = jnp.concatenate([att[c, j] for j in range(GROUP)], axis=1)
        for x in range(0, width, 512):
            part = jnp.dot(
                attended,
                weight[c * wide : (c + 1) * wide, x : x + 512],
                preferred_element_type=F32,
            )
            if c > 0:
                part = part + total[:, x : x + 512]
            if c < chunks - 1:
                total[:, x : x + 512] = part
            else:
                out_ref[:, x : x + 512] = (
                    residual[:, x : x + 512].astype(F32) + gate_rows[:, x : x + 512] * part
                ).astype(out_ref.dtype)

    def own_back(c):
        return pltpu.make_async_copy(
            att_send.at[c, mine], att.at[c, mine], own_sem.at[chunks + 1 + c]
        )

    scale = 1.0 / math.sqrt(HEAD_DIM)
    for c in range(chunks):

        def wait_chunk(o, carry, c=c):
            arrival(c, o).wait_recv()
            return carry

        lax.fori_loop(1, n, wait_chunk, 0)
        own_copy(c).wait()
        arrived = recv[c].reshape(n * slots, 3 * HEAD_DIM)
        rows_qkv = jnp.dot(pick[...], arrived, preferred_element_type=F32).astype(BF16)
        keys = rows_qkv[:, HEAD_DIM : 2 * HEAD_DIM]
        vals = rows_qkv[:, 2 * HEAD_DIM :]
        for b in range(GROUP):
            queries = rows_qkv[b * tile : (b + 1) * tile, :HEAD_DIM]
            scores = (
                lax.dot_general(
                    queries, keys, (((1,), (1,)), ((), ())), preferred_element_type=F32
                )
                * scale
                + bias[b * tile : (b + 1) * tile, :]
            )
            top = jnp.max(scores, axis=1, keepdims=True)
            weights = jnp.exp(scores - top)
            denominator = jnp.sum(weights, axis=1, keepdims=True)
            mixture = jnp.dot(weights.astype(BF16), vals, preferred_element_type=F32)
            att_send[c, b] = (mixture / denominator).astype(BF16)
        for o in range(1, GROUP):
            back_copy(c, o).start()
        own_back(c).start()
        if c > 0:
            project(c - 1)
    project(chunks - 1)

    def wait_sent(o, carry):
        meta_copy(o).wait_send()
        for c in range(chunks):
            copy(c, o).wait_send()
        return carry

    lax.fori_loop(1, n, wait_sent, 0)
    for c in range(chunks):
        for o in range(1, GROUP):
            back_copy(c, o).wait_send()


def shards(queries, keys, values, destination, row_clip, residual, gate, out_weight):
    n = lax.axis_size("tiles")
    tile, features = queries.shape
    width = residual.shape[1]
    chunks = features // (GROUP * HEAD_DIM)
    windows = n // GROUP
    slots = max(GROUP * (2 * tile // n), 16)
    window = GROUP * tile
    vmem = pl.BlockSpec(memory_space=pltpu.VMEM)
    anywhere = pl.BlockSpec(memory_space=pl.ANY)
    dma = pltpu.SemaphoreType.DMA
    return pl.pallas_call(
        functools.partial(kernel, n, slots),
        out_shape=jax.ShapeDtypeStruct((tile, width), BF16),
        in_specs=[vmem] * 6 + [anywhere] * 2,
        out_specs=vmem,
        scratch_shapes=[
            pltpu.VMEM((chunks, windows, GROUP, slots, 3 * HEAD_DIM), BF16),
            pltpu.VMEM((chunks, n, slots, 3 * HEAD_DIM), BF16),
            pltpu.VMEM((windows, 1, 128), jnp.int32),
            pltpu.VMEM((n, 1, 128), jnp.int32),
            pltpu.VMEM((window, n * slots), BF16),
            pltpu.VMEM((window, 128), F32),
            pltpu.VMEM((window, window), F32),
            pltpu.VMEM((chunks, GROUP, tile, HEAD_DIM), BF16),
            pltpu.VMEM((chunks, GROUP, tile, HEAD_DIM), BF16),
            pltpu.VMEM((tile, width), F32),
            pltpu.VMEM((tile, width), F32),
            pltpu.VMEM((features, width), BF16),
            pltpu.VMEM((tile, width), BF16),
            dma((chunks, n)),
            dma((chunks, n)),
            dma((n,)),
            dma((n,)),
            dma((chunks, GROUP)),
            dma((chunks, GROUP)),
            dma((2,)),
            dma((2 * chunks + 1,)),
        ],
        compiler_params=pltpu.CompilerParams(
            collective_id=0, has_side_effects=True, vmem_limit_bytes=50 * 1024 * 1024
        ),
    )(
        queries,
        keys,
        values,
        destination.reshape(1, tile),
        row_clip.reshape(1, tile),
        gate,
        residual,
        out_weight,
    )


def solution(mesh):
    rows = P("tiles", None)
    in_specs = (rows, rows, rows, P("tiles"), P("tiles"), rows, P(), P())
    return jax.shard_map(shards, mesh=mesh, in_specs=in_specs, out_specs=rows, check_vma=False)
```

```python
import functools
import math

import jax
import jax.numpy as jnp
from jax import lax
from jax.experimental import pallas as pl
from jax.experimental.pallas import tpu as pltpu
from jax.sharding import PartitionSpec as P

HEAD_DIM = 128
GROUP = 4
MESH = pl.DeviceIdType.MESH
F32 = jnp.float32
BF16 = jnp.bfloat16


def kernel(
    n,
    slots,
    q_hbm,
    k_hbm,
    v_hbm,
    dest_hbm,
    clip_hbm,
    gate_hbm,
    residual_hbm,
    weight_hbm,
    out_ref,
    q_ref,
    k_ref,
    v_ref,
    dest_ref,
    clip_ref,
    gate_ref,
    send,
    recv,
    meta_send,
    meta_recv,
    pick,
    clip_col,
    bias,
    att_send,
    att,
    total,
    gate_rows,
    weight,
    residual,
    send_sem,
    recv_sem,
    meta_send_sem,
    meta_recv_sem,
    back_send_sem,
    back_recv_sem,
    load_sem,
    own_sem,
):
    tile = q_ref.shape[0]
    chunks = q_ref.shape[1] // (GROUP * HEAD_DIM)
    wide = GROUP * HEAD_DIM
    window = GROUP * tile
    windows = n // GROUP
    me = lax.axis_index("tiles")
    my_window = me // GROUP
    mine = me % GROUP

    barrier = pltpu.get_barrier_semaphore()
    sources = (dest_hbm, clip_hbm, q_hbm, k_hbm, v_hbm, gate_hbm, residual_hbm, weight_hbm)
    targets = (dest_ref, clip_ref, q_ref, k_ref, v_ref, gate_ref, residual, weight)
    loads = [
        pltpu.make_async_copy(source, target, load_sem.at[i])
        for i, (source, target) in enumerate(zip(sources, targets))
    ]
    for load in loads[:5]:
        load.start()

    def greet(o, carry):
        pl.semaphore_signal(barrier, inc=1, device_id=((me + o) % n,), device_id_type=MESH)
        return carry

    lax.fori_loop(1, n, greet, 0)

    loads[0].wait()
    loads[1].wait()
    dest_row = dest_ref[...]
    win_row = lax.div(dest_row, jnp.int32(window))
    code_row = lax.rem(dest_row, jnp.int32(window)) + 1 + clip_ref[...] * 1024
    line = lax.broadcasted_iota(jnp.int32, (tile, tile), 0)
    lane = lax.broadcasted_iota(jnp.int32, (tile, tile), 1)
    eye = line == lane

    def to_column(row):
        wide_row = jnp.broadcast_to(row.astype(F32), (tile, tile))
        return jnp.sum(jnp.where(eye, wide_row, 0.0), axis=1, keepdims=True).astype(jnp.int32)

    win_col = to_column(win_row)
    code_col = to_column(code_row)
    same = win_col == win_row
    rank_row = jnp.sum(jnp.where(same & (line < lane), 1.0, 0.0), axis=0, keepdims=True)
    rank_col = jnp.sum(jnp.where(same & (lane < line), 1.0, 0.0), axis=1, keepdims=True)
    slot_row = win_row * slots + rank_row.astype(jnp.int32)
    slot_col = win_col * 128 + rank_col.astype(jnp.int32)

    spread = lax.broadcasted_iota(jnp.int32, (tile, 128), 1) % slots
    for w in range(windows):
        hit = slot_col == spread + w * 128
        codes = jnp.sum(jnp.where(hit, code_col.astype(F32), 0.0), axis=0, keepdims=True)
        meta_send[w] = codes.astype(jnp.int32)

    slot_line = lax.broadcasted_iota(jnp.int32, (windows * slots, tile), 0)
    place = jnp.where(slot_line == slot_row, 1.0, 0.0).astype(BF16)

    def order(i):
        return n // 2 + (1 - 2 * (i % 2)) * ((i + 1) // 2)

    def meta_copy(o):
        to = (me + o) % n
        return pltpu.make_async_remote_copy(
            src_ref=meta_send.at[to // GROUP],
            dst_ref=meta_recv.at[me],
            send_sem=meta_send_sem.at[o],
            recv_sem=meta_recv_sem.at[me],
            device_id=(to,),
            device_id_type=MESH,
        )

    def meta_arrival(o):
        come = (me + o) % n
        return pltpu.make_async_remote_copy(
            src_ref=meta_send.at[0],
            dst_ref=meta_recv.at[come],
            send_sem=meta_send_sem.at[o],
            recv_sem=meta_recv_sem.at[come],
            device_id=(come,),
            device_id_type=MESH,
        )

    def copy(c, o):
        to = (me + o) % n
        return pltpu.make_async_remote_copy(
            src_ref=send.at[c, to // GROUP, to % GROUP],
            dst_ref=recv.at[c, me],
            send_sem=send_sem.at[c, o],
            recv_sem=recv_sem.at[c, me],
            device_id=(to,),
            device_id_type=MESH,
        )

    def arrival(c, o):
        come = (me + o) % n
        return pltpu.make_async_remote_copy(
            src_ref=send.at[c, 0, 0],
            dst_ref=recv.at[c, come],
            send_sem=send_sem.at[c, o],
            recv_sem=recv_sem.at[c, come],
            device_id=(come,),
            device_id_type=MESH,
        )

    def own_copy(c):
        return pltpu.make_async_copy(
            send.at[c, my_window, mine], recv.at[c, me], own_sem.at[c]
        )

    own_meta = pltpu.make_async_copy(meta_send.at[my_window], meta_recv.at[me], own_sem.at[chunks])

    for c in range(chunks):
        for t, ref in enumerate((q_ref, k_ref, v_ref)):
            if c == 0:
                loads[2 + t].wait()
            packed = jnp.dot(
                place, ref[:, c * wide : (c + 1) * wide], preferred_element_type=F32
            ).astype(BF16)
            for j in range(GROUP):
                part = packed[:, j * HEAD_DIM : (j + 1) * HEAD_DIM]
                send[c, :, j, :, t * HEAD_DIM : (t + 1) * HEAD_DIM] = part.reshape(
                    windows, slots, HEAD_DIM
                )
        if c == 0:
            pl.semaphore_wait(barrier, n - 1)

        def start_chunk(i, carry, c=c):
            copy(c, order(i)).start()
            return carry

        lax.fori_loop(0, n - 1, start_chunk, 0)
        own_copy(c).start()
        if c == 0:

            def start_meta(o, carry):
                meta_copy(o).start()
                return carry

            lax.fori_loop(1, n, start_meta, 0)
            own_meta.start()

    for load in loads[5:]:
        load.start()

    def wait_meta(o, carry):
        meta_arrival(o).wait_recv()
        return carry

    lax.fori_loop(1, n, wait_meta, 0)
    own_meta.wait()
    per_row = 128 // slots
    lane_block = lax.broadcasted_iota(jnp.int32, (1, 128), 1) // slots
    rows = []
    for g in range(n // per_row):
        row = jnp.zeros((1, 128), jnp.int32)
        for i in range(per_row):
            row = jnp.where(lane_block == i, meta_recv[g * per_row + i], row)
        rows.append(row)
    for b in range(GROUP):
        spot = lax.broadcasted_iota(jnp.int32, (tile, 128), 0) + (b * tile + 1)
        sums = jnp.zeros((tile, 128), F32)
        for g, row in enumerate(rows):
            hit = spot == (row & 1023)
            pick[b * tile : (b + 1) * tile, g * 128 : (g + 1) * 128] = jnp.where(
                hit, 1.0, 0.0
            ).astype(BF16)
            sums = sums + jnp.where(hit, (row >> 10).astype(F32), 0.0)
        column = jnp.sum(sums, axis=1, keepdims=True)
        clip_col[b * tile : (b + 1) * tile, :] = jnp.broadcast_to(column, (tile, 128))
    for b in range(GROUP):
        key_clip = jnp.sum(
            jnp.where(eye, clip_col[b * tile : (b + 1) * tile, :], 0.0), axis=0, keepdims=True
        )
        for a in range(GROUP):
            query_clip = clip_col[a * tile : (a + 1) * tile, :]
            bias[a * tile : (a + 1) * tile, b * tile : (b + 1) * tile] = jnp.where(
                query_clip == key_clip, 0.0, -1e30
            )

    loads[5].wait()
    clips = gate_ref.shape[0]
    my_clip = clip_col[pl.ds(pl.multiple_of(mine * tile, tile), tile), :]
    lookup = jnp.where(
        my_clip[:, :clips] == lax.broadcasted_iota(jnp.int32, (tile, clips), 1).astype(F32), 1.0, 0.0
    )
    width = out_ref.shape[1]
    for x in range(0, width, 512):
        gate_rows[:, x : x + 512] = jnp.dot(
            lookup,
            gate_ref[:, x : x + 512],
            precision=lax.Precision.HIGHEST,
            preferred_element_type=F32,
        )
    loads[6].wait()
    loads[7].wait()

    def back_copy(c, o):
        to = (mine + o) % GROUP
        return pltpu.make_async_remote_copy(
            src_ref=att_send.at[c, to],
            dst_ref=att.at[c, mine],
            send_sem=back_send_sem.at[c, o],
            recv_sem=back_recv_sem.at[c, mine],
            device_id=(my_window * GROUP + to,),
            device_id_type=MESH,
        )

    def back_arrival(c, o):
        come = (mine + o) % GROUP
        return pltpu.make_async_remote_copy(
            src_ref=att_send.at[c, 0],
            dst_ref=att.at[c, come],
            send_sem=back_send_sem.at[c, o],
            recv_sem=back_recv_sem.at[c, come],
            device_id=(my_window * GROUP + come,),
            device_id_type=MESH,
        )

    def project(c):
        for o in range(1, GROUP):
            back_arrival(c, o).wait_recv()
        own_back(c).wait()
        attended = jnp.concatenate([att[c, j] for j in range(GROUP)], axis=1)
        for x in range(0, width, 512):
            part = jnp.dot(
                attended,
                weight[c * wide : (c + 1) * wide, x : x + 512],
                preferred_element_type=F32,
            )
            if c > 0:
                part = part + total[:, x : x + 512]
            if c < chunks - 1:
                total[:, x : x + 512] = part
            else:
                out_ref[:, x : x + 512] = (
                    residual[:, x : x + 512].astype(F32) + gate_rows[:, x : x + 512] * part
                ).astype(out_ref.dtype)

    def own_back(c):
        return pltpu.make_async_copy(
            att_send.at[c, mine], att.at[c, mine], own_sem.at[chunks + 1 + c]
        )

    scale = 1.0 / math.sqrt(HEAD_DIM)
    for c in range(chunks):

        def wait_chunk(o, carry, c=c):
            arrival(c, o).wait_recv()
            return carry

        lax.fori_loop(1, n, wait_chunk, 0)
        own_copy(c).wait()
        arrived = recv[c].reshape(n * slots, 3 * HEAD_DIM)
        rows_qkv = jnp.dot(pick[...], arrived, preferred_element_type=F32).astype(BF16)
        keys = rows_qkv[:, HEAD_DIM : 2 * HEAD_DIM]
        vals = rows_qkv[:, 2 * HEAD_DIM :]
        for b in range(GROUP):
            queries = rows_qkv[b * tile : (b + 1) * tile, :HEAD_DIM]
            scores = (
                lax.dot_general(
                    queries, keys, (((1,), (1,)), ((), ())), preferred_element_type=F32
                )
                * scale
                + bias[b * tile : (b + 1) * tile, :]
            )
            top = jnp.max(scores, axis=1, keepdims=True)
            weights = jnp.exp(scores - top)
            denominator = jnp.sum(weights, axis=1, keepdims=True)
            mixture = jnp.dot(weights.astype(BF16), vals, preferred_element_type=F32)
            att_send[c, b] = (mixture / denominator).astype(BF16)
        for o in range(1, GROUP):
            back_copy(c, o).start()
        own_back(c).start()
        if c > 0:
            project(c - 1)
    project(chunks - 1)

    def wait_sent(o, carry):
        meta_copy(o).wait_send()
        for c in range(chunks):
            copy(c, o).wait_send()
        return carry

    lax.fori_loop(1, n, wait_sent, 0)
    for c in range(chunks):
        for o in range(1, GROUP):
            back_copy(c, o).wait_send()


def shards(queries, keys, values, destination, row_clip, residual, gate, out_weight):
    n = lax.axis_size("tiles")
    tile, features = queries.shape
    width = residual.shape[1]
    chunks = features // (GROUP * HEAD_DIM)
    windows = n // GROUP
    slots = max(GROUP * (2 * tile // n), 16)
    window = GROUP * tile
    vmem = pl.BlockSpec(memory_space=pltpu.VMEM)
    anywhere = pl.BlockSpec(memory_space=pltpu.HBM)
    dma = pltpu.SemaphoreType.DMA
    return pl.pallas_call(
        functools.partial(kernel, n, slots),
        out_shape=jax.ShapeDtypeStruct((tile, width), BF16),
        in_specs=[anywhere] * 8,
        out_specs=vmem,
        scratch_shapes=[
            pltpu.VMEM((tile, features), BF16),
            pltpu.VMEM((tile, features), BF16),
            pltpu.VMEM((tile, features), BF16),
            pltpu.VMEM((1, tile), jnp.int32),
            pltpu.VMEM((1, tile), jnp.int32),
            pltpu.VMEM(gate.shape, F32),
            pltpu.VMEM((chunks, windows, GROUP, slots, 3 * HEAD_DIM), BF16),
            pltpu.VMEM((chunks, n, slots, 3 * HEAD_DIM), BF16),
            pltpu.VMEM((windows, 1, 128), jnp.int32),
            pltpu.VMEM((n, 1, 128), jnp.int32),
            pltpu.VMEM((window, n * slots), BF16),
            pltpu.VMEM((window, 128), F32),
            pltpu.VMEM((window, window), F32),
            pltpu.VMEM((chunks, GROUP, tile, HEAD_DIM), BF16),
            pltpu.VMEM((chunks, GROUP, tile, HEAD_DIM), BF16),
            pltpu.VMEM((tile, width), F32),
            pltpu.VMEM((tile, width), F32),
            pltpu.VMEM((features, width), BF16),
            pltpu.VMEM((tile, width), BF16),
            dma((chunks, n)),
            dma((chunks, n)),
            dma((n,)),
            dma((n,)),
            dma((chunks, GROUP)),
            dma((chunks, GROUP)),
            dma((8,)),
            dma((2 * chunks + 1,)),
        ],
        compiler_params=pltpu.CompilerParams(
            collective_id=0, has_side_effects=True, vmem_limit_bytes=60 * 1024 * 1024
        ),
    )(
        queries,
        keys,
        values,
        destination.reshape(1, tile),
        row_clip.reshape(1, tile),
        gate,
        residual,
        out_weight,
    )


def solution(mesh):
    rows = P("tiles", None)
    in_specs = (rows, rows, rows, P("tiles"), P("tiles"), rows, P(), P())
    return jax.shard_map(shards, mesh=mesh, in_specs=in_specs, out_specs=rows, check_vma=False)
```

```python
import functools
import math

import jax
import jax.numpy as jnp
from jax import lax
from jax.experimental import pallas as pl
from jax.experimental.pallas import tpu as pltpu
from jax.sharding import PartitionSpec as P

HEAD_DIM = 128
GROUP = 4
MESH = pl.DeviceIdType.MESH
F32 = jnp.float32
BF16 = jnp.bfloat16


def kernel(
    n,
    slots,
    q_hbm,
    k_hbm,
    v_hbm,
    dest_hbm,
    clip_hbm,
    gate_hbm,
    residual_hbm,
    weight_hbm,
    out_hbm,
    q_ref,
    k_ref,
    v_ref,
    dest_ref,
    clip_ref,
    gate_ref,
    send,
    recv,
    meta_send,
    meta_recv,
    pick,
    clip_col,
    bias,
    att_send,
    att,
    total,
    gate_rows,
    weight,
    residual,
    out_ref,
    store_sem,
    send_sem,
    recv_sem,
    meta_send_sem,
    meta_recv_sem,
    back_send_sem,
    back_recv_sem,
    load_sem,
    own_sem,
):
    tile = q_ref.shape[0]
    chunks = q_ref.shape[1] // (GROUP * HEAD_DIM)
    wide = GROUP * HEAD_DIM
    window = GROUP * tile
    windows = n // GROUP
    me = lax.axis_index("tiles")
    my_window = me // GROUP
    mine = me % GROUP

    barrier = pltpu.get_barrier_semaphore()
    sources = (dest_hbm, clip_hbm, q_hbm, k_hbm, v_hbm, gate_hbm, residual_hbm, weight_hbm)
    targets = (dest_ref, clip_ref, q_ref, k_ref, v_ref, gate_ref, residual, weight)
    loads = [
        pltpu.make_async_copy(source, target, load_sem.at[i])
        for i, (source, target) in enumerate(zip(sources, targets))
    ]
    for load in loads[:5]:
        load.start()

    def greet(o, carry):
        pl.semaphore_signal(barrier, inc=1, device_id=((me + o) % n,), device_id_type=MESH)
        return carry

    lax.fori_loop(1, n, greet, 0)

    loads[0].wait()
    loads[1].wait()
    dest_row = dest_ref[...]
    win_row = lax.div(dest_row, jnp.int32(window))
    code_row = lax.rem(dest_row, jnp.int32(window)) + 1 + clip_ref[...] * 1024
    line = lax.broadcasted_iota(jnp.int32, (tile, tile), 0)
    lane = lax.broadcasted_iota(jnp.int32, (tile, tile), 1)
    eye = line == lane

    def to_column(row):
        wide_row = jnp.broadcast_to(row.astype(F32), (tile, tile))
        return jnp.sum(jnp.where(eye, wide_row, 0.0), axis=1, keepdims=True).astype(jnp.int32)

    win_col = to_column(win_row)
    code_col = to_column(code_row)
    same = win_col == win_row
    rank_row = jnp.sum(jnp.where(same & (line < lane), 1.0, 0.0), axis=0, keepdims=True)
    rank_col = jnp.sum(jnp.where(same & (lane < line), 1.0, 0.0), axis=1, keepdims=True)
    slot_row = win_row * slots + rank_row.astype(jnp.int32)
    slot_col = win_col * 128 + rank_col.astype(jnp.int32)

    spread = lax.broadcasted_iota(jnp.int32, (tile, 128), 1) % slots
    for w in range(windows):
        hit = slot_col == spread + w * 128
        codes = jnp.sum(jnp.where(hit, code_col.astype(F32), 0.0), axis=0, keepdims=True)
        meta_send[w] = codes.astype(jnp.int32)

    slot_line = lax.broadcasted_iota(jnp.int32, (windows * slots, tile), 0)
    place = jnp.where(slot_line == slot_row, 1.0, 0.0).astype(BF16)

    def meta_copy(o):
        to = (me + o) % n
        return pltpu.make_async_remote_copy(
            src_ref=meta_send.at[to // GROUP],
            dst_ref=meta_recv.at[me],
            send_sem=meta_send_sem.at[o],
            recv_sem=meta_recv_sem.at[me],
            device_id=(to,),
            device_id_type=MESH,
        )

    def meta_arrival(o):
        come = (me + o) % n
        return pltpu.make_async_remote_copy(
            src_ref=meta_send.at[0],
            dst_ref=meta_recv.at[come],
            send_sem=meta_send_sem.at[o],
            recv_sem=meta_recv_sem.at[come],
            device_id=(come,),
            device_id_type=MESH,
        )

    def copy(c, o):
        to = (me + o) % n
        return pltpu.make_async_remote_copy(
            src_ref=send.at[c, to // GROUP, to % GROUP],
            dst_ref=recv.at[c, me],
            send_sem=send_sem.at[c, o],
            recv_sem=recv_sem.at[c, me],
            device_id=(to,),
            device_id_type=MESH,
        )

    def arrival(c, o):
        come = (me + o) % n
        return pltpu.make_async_remote_copy(
            src_ref=send.at[c, 0, 0],
            dst_ref=recv.at[c, come],
            send_sem=send_sem.at[c, o],
            recv_sem=recv_sem.at[c, come],
            device_id=(come,),
            device_id_type=MESH,
        )

    def own_copy(c):
        return pltpu.make_async_copy(
            send.at[c, my_window, mine], recv.at[c, me], own_sem.at[c]
        )

    own_meta = pltpu.make_async_copy(meta_send.at[my_window], meta_recv.at[me], own_sem.at[chunks])

    for c in range(chunks):
        for t, ref in enumerate((q_ref, k_ref, v_ref)):
            if c == 0:
                loads[2 + t].wait()
            packed = jnp.dot(
                place, ref[:, c * wide : (c + 1) * wide], preferred_element_type=F32
            ).astype(BF16)
            for j in range(GROUP):
                part = packed[:, j * HEAD_DIM : (j + 1) * HEAD_DIM]
                send[c, :, j, :, t * HEAD_DIM : (t + 1) * HEAD_DIM] = part.reshape(
                    windows, slots, HEAD_DIM
                )
        if c == 0:
            pl.semaphore_wait(barrier, n - 1)

        def start_chunk(i, carry, c=c):
            copy(c, i).start()
            return carry

        lax.fori_loop(1, n, start_chunk, 0)
        own_copy(c).start()
        if c == 0:

            def start_meta(o, carry):
                meta_copy(o).start()
                return carry

            lax.fori_loop(1, n, start_meta, 0)
            own_meta.start()

    for load in loads[5:]:
        load.start()

    def wait_meta(o, carry):
        meta_arrival(o).wait_recv()
        return carry

    lax.fori_loop(1, n, wait_meta, 0)
    own_meta.wait()
    per_row = 128 // slots
    lane_block = lax.broadcasted_iota(jnp.int32, (1, 128), 1) // slots
    rows = []
    for g in range(n // per_row):
        row = jnp.zeros((1, 128), jnp.int32)
        for i in range(per_row):
            row = jnp.where(lane_block == i, meta_recv[g * per_row + i], row)
        rows.append(row)
    for b in range(GROUP):
        spot = lax.broadcasted_iota(jnp.int32, (tile, 128), 0) + (b * tile + 1)
        sums = jnp.zeros((tile, 128), F32)
        for g, row in enumerate(rows):
            hit = spot == (row & 1023)
            pick[b * tile : (b + 1) * tile, g * 128 : (g + 1) * 128] = jnp.where(
                hit, 1.0, 0.0
            ).astype(BF16)
            sums = sums + jnp.where(hit, (row >> 10).astype(F32), 0.0)
        column = jnp.sum(sums, axis=1, keepdims=True)
        clip_col[b * tile : (b + 1) * tile, :] = jnp.broadcast_to(column, (tile, 128))
    for b in range(GROUP):
        key_clip = jnp.sum(
            jnp.where(eye, clip_col[b * tile : (b + 1) * tile, :], 0.0), axis=0, keepdims=True
        )
        for a in range(GROUP):
            query_clip = clip_col[a * tile : (a + 1) * tile, :]
            bias[a * tile : (a + 1) * tile, b * tile : (b + 1) * tile] = jnp.where(
                query_clip == key_clip, 0.0, -1e30
            )

    loads[5].wait()
    clips = gate_ref.shape[0]
    my_clip = clip_col[pl.ds(pl.multiple_of(mine * tile, tile), tile), :]
    lookup = jnp.where(
        my_clip[:, :clips] == lax.broadcasted_iota(jnp.int32, (tile, clips), 1).astype(F32), 1.0, 0.0
    )
    width = out_ref.shape[1]
    for x in range(0, width, 512):
        gate_rows[:, x : x + 512] = jnp.dot(
            lookup,
            gate_ref[:, x : x + 512],
            precision=lax.Precision.HIGHEST,
            preferred_element_type=F32,
        )
    loads[6].wait()
    loads[7].wait()

    def back_copy(c, o):
        to = (mine + o) % GROUP
        return pltpu.make_async_remote_copy(
            src_ref=att_send.at[c, to],
            dst_ref=att.at[c, mine],
            send_sem=back_send_sem.at[c, o],
            recv_sem=back_recv_sem.at[c, mine],
            device_id=(my_window * GROUP + to,),
            device_id_type=MESH,
        )

    def back_arrival(c, o):
        come = (mine + o) % GROUP
        return pltpu.make_async_remote_copy(
            src_ref=att_send.at[c, 0],
            dst_ref=att.at[c, come],
            send_sem=back_send_sem.at[c, o],
            recv_sem=back_recv_sem.at[c, come],
            device_id=(my_window * GROUP + come,),
            device_id_type=MESH,
        )

    def store(x):
        return pltpu.make_async_copy(
            out_ref.at[:, x : x + 512], out_hbm.at[:, x : x + 512], store_sem.at[x // 512]
        )

    def project(c):
        for o in range(1, GROUP):
            back_arrival(c, o).wait_recv()
        own_back(c).wait()
        attended = jnp.concatenate([att[c, j] for j in range(GROUP)], axis=1)
        for x in range(0, width, 512):
            part = jnp.dot(
                attended,
                weight[c * wide : (c + 1) * wide, x : x + 512],
                preferred_element_type=F32,
            )
            if c > 0:
                part = part + total[:, x : x + 512]
            if c < chunks - 1:
                total[:, x : x + 512] = part
            else:
                out_ref[:, x : x + 512] = (
                    residual[:, x : x + 512].astype(F32) + gate_rows[:, x : x + 512] * part
                ).astype(out_ref.dtype)
                store(x).start()

    def own_back(c):
        return pltpu.make_async_copy(
            att_send.at[c, mine], att.at[c, mine], own_sem.at[chunks + 1 + c]
        )

    scale = 1.0 / math.sqrt(HEAD_DIM)
    for c in range(chunks):

        def wait_chunk(o, carry, c=c):
            arrival(c, o).wait_recv()
            return carry

        lax.fori_loop(1, n, wait_chunk, 0)
        own_copy(c).wait()
        arrived = recv[c].reshape(n * slots, 3 * HEAD_DIM)
        rows_qkv = jnp.dot(pick[...], arrived, preferred_element_type=F32).astype(BF16)
        keys = rows_qkv[:, HEAD_DIM : 2 * HEAD_DIM]
        vals = rows_qkv[:, 2 * HEAD_DIM :]
        for b in range(GROUP):
            queries = rows_qkv[b * tile : (b + 1) * tile, :HEAD_DIM]
            scores = (
                lax.dot_general(
                    queries, keys, (((1,), (1,)), ((), ())), preferred_element_type=F32
                )
                * scale
                + bias[b * tile : (b + 1) * tile, :]
            )
            top = jnp.max(scores, axis=1, keepdims=True)
            weights = jnp.exp(scores - top)
            denominator = jnp.sum(weights, axis=1, keepdims=True)
            mixture = jnp.dot(weights.astype(BF16), vals, preferred_element_type=F32)
            att_send[c, b] = (mixture / denominator).astype(BF16)
        for o in range(1, GROUP):
            back_copy(c, o).start()
        own_back(c).start()
        if c > 0:
            project(c - 1)
    project(chunks - 1)

    def wait_sent(o, carry):
        meta_copy(o).wait_send()
        for c in range(chunks):
            copy(c, o).wait_send()
        return carry

    lax.fori_loop(1, n, wait_sent, 0)
    for x in range(0, width, 512):
        store(x).wait()
    for c in range(chunks):
        for o in range(1, GROUP):
            back_copy(c, o).wait_send()


def shards(queries, keys, values, destination, row_clip, residual, gate, out_weight):
    n = lax.axis_size("tiles")
    tile, features = queries.shape
    width = residual.shape[1]
    chunks = features // (GROUP * HEAD_DIM)
    windows = n // GROUP
    slots = max(GROUP * (2 * tile // n), 16)
    window = GROUP * tile
    anywhere = pl.BlockSpec(memory_space=pltpu.HBM)
    dma = pltpu.SemaphoreType.DMA
    return pl.pallas_call(
        functools.partial(kernel, n, slots),
        out_shape=jax.ShapeDtypeStruct((tile, width), BF16),
        in_specs=[anywhere] * 8,
        out_specs=anywhere,
        scratch_shapes=[
            pltpu.VMEM((tile, features), BF16),
            pltpu.VMEM((tile, features), BF16),
            pltpu.VMEM((tile, features), BF16),
            pltpu.VMEM((1, tile), jnp.int32),
            pltpu.VMEM((1, tile), jnp.int32),
            pltpu.VMEM(gate.shape, F32),
            pltpu.VMEM((chunks, windows, GROUP, slots, 3 * HEAD_DIM), BF16),
            pltpu.VMEM((chunks, n, slots, 3 * HEAD_DIM), BF16),
            pltpu.VMEM((windows, 1, 128), jnp.int32),
            pltpu.VMEM((n, 1, 128), jnp.int32),
            pltpu.VMEM((window, n * slots), BF16),
            pltpu.VMEM((window, 128), F32),
            pltpu.VMEM((window, window), F32),
            pltpu.VMEM((chunks, GROUP, tile, HEAD_DIM), BF16),
            pltpu.VMEM((chunks, GROUP, tile, HEAD_DIM), BF16),
            pltpu.VMEM((tile, width), F32),
            pltpu.VMEM((tile, width), F32),
            pltpu.VMEM((features, width), BF16),
            pltpu.VMEM((tile, width), BF16),
            pltpu.VMEM((tile, width), BF16),
            dma((width // 512,)),
            dma((chunks, n)),
            dma((chunks, n)),
            dma((n,)),
            dma((n,)),
            dma((chunks, GROUP)),
            dma((chunks, GROUP)),
            dma((8,)),
            dma((2 * chunks + 1,)),
        ],
        compiler_params=pltpu.CompilerParams(
            collective_id=0, has_side_effects=True, vmem_limit_bytes=60 * 1024 * 1024
        ),
    )(
        queries,
        keys,
        values,
        destination.reshape(1, tile),
        row_clip.reshape(1, tile),
        gate,
        residual,
        out_weight,
    )


def solution(mesh):
    rows = P("tiles", None)
    in_specs = (rows, rows, rows, P("tiles"), P("tiles"), rows, P(), P())
    return jax.shard_map(shards, mesh=mesh, in_specs=in_specs, out_specs=rows, check_vma=False)
```
